32 devices in a mesh: row: 8 (over y, x, core), col: 4 (over z).
Axes of the slice: x: 2, y: 2, z: 4, core: 2. Of those that a mesh axis runs over, the one named last changes fastest.
Arguments:
- adjoint: float32 [3, 512, 256, 256], P(None, 'row', 'col'), may hold values from -6 to 6
- gradients: bfloat16 [9, 384, 768, 384], P(None, 'row', 'col'), may hold values from -6 to 6
Outputs:
- forcing: float32 [3, 512, 256, 256], P(None, 'row', 'col')
The draws below stay inside these ranges and needn't reach their ends.
All inputs are finite; a program needn't handle non-finite values.
Results may differ from the reference program's by a relative error of at most 0.0003.
Values sent between devices are 32-bit elements; how exact they have to be, the bound alone decides.
A program may use at most 384 MiB of HBM per device.

```python
import math
import jax
import jax.numpy as jnp
from jax import lax

KR = 256
KT = 512
KZ = 256
NR = 384
NT = 768
NZ = 384


def shard_levels(key, shape, pieces, smallest, top_value):
    level, own = 1.0, jax.random.fold_in(key, 6)
    for dim, shards_of in pieces:
        heights = jnp.exp(jax.random.uniform(jax.random.fold_in(own, dim), (shards_of,), jnp.float32, smallest / len(pieces), top_value / len(pieces)))
        level = level * jnp.repeat(heights, shape[dim] // shards_of).reshape([-1 if axis == dim else 1 for axis in range(len(shape))])
    return level


def scatter_about(own_key, shape, scale, most, cuts=(), kind=jnp.bfloat16):
    values = scale * jax.random.normal(own_key, shape, jnp.float32)
    if cuts:
        values = values * shard_levels(own_key, shape, cuts, -0.22, 0.18)
    return jnp.clip(values, -most, most).astype(kind)


def setup_inputs(seed: int = 0) -> dict:
    key_of = jax.random.split(jax.random.key(seed), 3)
    return {
        "adjoint": scatter_about(key_of[0], (3, KT, KZ, KR), 1.0, 6.0, ((1, 8), (2, 4)), jnp.float32),
        "gradients": scatter_about(key_of[1], (9, NR, NT, NZ), 1.0, 6.0, ((1, 8), (2, 4))),
    }


def wave_table(points, modes):
    positions = jnp.arange(points, dtype=jnp.int32)[:, None]
    indices = jnp.arange(modes, dtype=jnp.int32)[None, :]
    wavenumber = (indices + 1) // 2
    angles = (positions * wavenumber % points).astype(jnp.float32) * (2.0 * math.pi / points)
    return jnp.where(indices % 2 == 1, jnp.cos(angles), jnp.where(indices == 0, jnp.ones_like(angles), jnp.sin(angles)))

def fourier_inverse(points, modes):
    return wave_table(points, modes) * (1.0 / math.sqrt(modes))

def fourier_forward(points, modes):
    indices = jnp.arange(modes, dtype=jnp.int32)
    weights = jnp.where(indices == 0, 1.0, 2.0).astype(jnp.float32) * (math.sqrt(modes) / points)
    return wave_table(points, modes).T * weights[:, None]

def cosine_table(points, modes):
    positions = jnp.arange(points, dtype=jnp.int32)[:, None]
    indices = jnp.arange(modes, dtype=jnp.int32)[None, :]
    angles = (indices * (2 * positions + 1) % (4 * points)).astype(jnp.float32) * (math.pi / (2 * points))
    return jnp.cos(angles)

def chebyshev_inverse(points, modes):
    return cosine_table(points, modes) * (1.0 / math.sqrt(modes))

def chebyshev_forward(points, modes):
    indices = jnp.arange(modes, dtype=jnp.int32)
    weights = jnp.where(indices == 0, 1.0, 2.0).astype(jnp.float32) * (math.sqrt(modes) / points)
    return cosine_table(points, modes).T * weights[:, None]

def reference(adjoint, gradients):
    highest = lax.Precision.HIGHEST
    radial = jnp.einsum('ftzk,jk->fjtz', adjoint, chebyshev_inverse(NR, KR), precision=highest)
    theta_inverse = fourier_inverse(NT, KT)
    axial_inverse = fourier_inverse(NZ, KZ)
    theta_forward = fourier_forward(NT, KT)
    axial_forward = fourier_forward(NZ, KZ)

    def one_shell(position):
        shell = lax.dynamic_index_in_dim(radial, position, 1, keepdims=False)
        shell_grad = lax.dynamic_index_in_dim(gradients, position, 1, keepdims=False)
        azimuthal = jnp.einsum('ftz,st->fsz', shell, theta_inverse, precision=highest)
        velocity = jnp.einsum('fsz,qz->fsq', azimuthal, axial_inverse, precision=highest)
        outputs = []
        for target in range(3):
            total = shell_grad[target].astype(jnp.float32) * velocity[0]
            for source in range(1, 3):
                total = total + shell_grad[3 * source + target].astype(jnp.float32) * velocity[source]
            outputs.append(total)
        product = jnp.stack(outputs)
        axial = jnp.einsum('fsq,zq->fsz', product, axial_forward, precision=highest)
        return jnp.einsum('fsz,ts->ftz', axial, theta_forward, precision=highest)
    shells = lax.map(one_shell, jnp.arange(NR, dtype=jnp.int32))
    return jnp.einsum('jftz,kj->ftzk', shells, chebyshev_forward(NR, KR), precision=highest)
```

```python
import functools
import math

import jax
import jax.numpy as jnp
from jax import lax
from jax.experimental import pallas as pl
from jax.experimental.pallas import tpu as pltpu
from jax.sharding import PartitionSpec as P

KR = 256
KT = 512
KZ = 256
NR = 384
NT = 768
NZ = 384


def wave_table(points, modes):
    positions = jnp.arange(points, dtype=jnp.int32)[:, None]
    indices = jnp.arange(modes, dtype=jnp.int32)[None, :]
    wavenumber = (indices + 1) // 2
    angles = (positions * wavenumber % points).astype(jnp.float32) * (2.0 * math.pi / points)
    return jnp.where(
        indices % 2 == 1,
        jnp.cos(angles),
        jnp.where(indices == 0, jnp.ones_like(angles), jnp.sin(angles)),
    )


def fourier_inverse(points, modes):
    return wave_table(points, modes) * (1.0 / math.sqrt(modes))


def fourier_forward(points, modes):
    indices = jnp.arange(modes, dtype=jnp.int32)
    weights = jnp.where(indices == 0, 1.0, 2.0).astype(jnp.float32) * (math.sqrt(modes) / points)
    return wave_table(points, modes).T * weights[:, None]


def cosine_table(points, modes):
    positions = jnp.arange(points, dtype=jnp.int32)[:, None]
    indices = jnp.arange(modes, dtype=jnp.int32)[None, :]
    angles = (indices * (2 * positions + 1) % (4 * points)).astype(jnp.float32) * (
        math.pi / (2 * points)
    )
    return jnp.cos(angles)


def chebyshev_inverse(points, modes):
    return cosine_table(points, modes) * (1.0 / math.sqrt(modes))


def chebyshev_forward(points, modes):
    indices = jnp.arange(modes, dtype=jnp.int32)
    weights = jnp.where(indices == 0, 1.0, 2.0).astype(jnp.float32) * (math.sqrt(modes) / points)
    return cosine_table(points, modes).T * weights[:, None]


MESH = pl.DeviceIdType.MESH
HIGH = lax.Precision.HIGH


def exchange_kernel(plans, *refs):
    parts = len(plans)
    sources, targets = refs[:parts], refs[parts : 2 * parts]
    send_sem, recv_sem, local_sem = refs[2 * parts :]
    barrier = pltpu.get_barrier_semaphore()
    total = 0
    for axis, count, _ in plans:
        me = lax.axis_index(axis)
        for step in range(1, count):
            peer = lax.rem(me + step, count)
            pl.semaphore_signal(barrier, inc=1, device_id={axis: peer}, device_id_type=MESH)
            total += 1
    pl.semaphore_wait(barrier, total)
    copies = []
    slot = 0
    for number, (axis, count, width) in enumerate(plans):
        me = lax.axis_index(axis)
        source, target = sources[number], targets[number]

        def piece(peer):
            if width is None:
                return source.at[peer]
            return source.at[:, pl.ds(pl.multiple_of(peer * width, 128), width)]

        for step in range(1, count):
            peer = lax.rem(me + step, count)
            copy = pltpu.make_async_remote_copy(
                src_ref=piece(peer),
                dst_ref=target.at[me],
                send_sem=send_sem.at[slot],
                recv_sem=recv_sem.at[slot],
                device_id={axis: peer},
                device_id_type=MESH,
            )
            copy.start()
            copies.append(copy)
            slot += 1
        own = pltpu.make_async_copy(piece(me), target.at[me], local_sem.at[number])
        own.start()
        copies.append(own)
    for copy in copies:
        copy.wait()


def exchange(ident, *parts):
    plans, shapes, total = [], [], 0
    for array, axis, width in parts:
        count = lax.axis_size(axis)
        total += count - 1
        plans.append((axis, count, width))
        shape = array.shape if width is None else (count, array.shape[0], width)
        shapes.append(jax.ShapeDtypeStruct(shape, array.dtype))
    return pl.pallas_call(
        functools.partial(exchange_kernel, tuple(plans)),
        out_shape=shapes,
        in_specs=[pl.BlockSpec(memory_space=pl.ANY)] * len(parts),
        out_specs=[pl.BlockSpec(memory_space=pl.ANY)] * len(parts),
        scratch_shapes=[
            pltpu.SemaphoreType.DMA((total,)),
            pltpu.SemaphoreType.DMA((total,)),
            pltpu.SemaphoreType.DMA((len(parts),)),
        ],
        compiler_params=pltpu.CompilerParams(collective_id=ident, has_side_effects=True),
    )(*[array for array, _, _ in parts])


def per_device(adjoint, gradients):
    kt_local = adjoint.shape[1]
    kz_local = adjoint.shape[2]
    rows_here = gradients.shape[1]
    columns_here = gradients.shape[2]
    row_count = lax.axis_size("row")
    col_count = lax.axis_size("col")
    width = rows_here * kz_local
    theta_inverse = fourier_inverse(NT, KT)
    axial_inverse = fourier_inverse(NZ, KZ)
    theta_forward = fourier_forward(NT, KT)
    axial_forward = fourier_forward(NZ, KZ)
    radial_forward = chebyshev_forward(NR, KR)
    radial_inverse = chebyshev_inverse(NR, KR)

    def first(f):
        radial = jnp.einsum("tzk,jk->tjz", adjoint[f], radial_inverse, precision=HIGH)
        return radial.reshape(kt_local, NR * kz_local), "row", width

    def second(gathered):
        turned = jnp.einsum("ka,sk->sa", gathered.reshape(KT, width), theta_inverse, precision=HIGH)
        return turned.reshape(col_count, columns_here, width), "col", None

    def third(arrived):
        layered = arrived.reshape(col_count, columns_here, rows_here, kz_local)
        ordered = jnp.transpose(layered, (1, 2, 0, 3)).reshape(columns_here, rows_here, KZ)
        return jnp.einsum("srk,qk->rsq", ordered, axial_inverse, precision=HIGH)

    (a0,) = exchange(1, first(0))
    a1, b0 = exchange(2, first(1), second(a0))
    a2, b1 = exchange(3, first(2), second(a1))
    (b2,) = exchange(4, second(a2))
    velocity = [third(b0), third(b1), third(b2)]

    def fourth(target):
        total = gradients[target].astype(jnp.float32) * velocity[0]
        for source in range(1, 3):
            total = total + gradients[3 * source + target].astype(jnp.float32) * velocity[source]
        axial = jnp.einsum("rsq,kq->srk", total, axial_forward, precision=HIGH)
        layered = axial.reshape(columns_here, rows_here, col_count, kz_local)
        returning = jnp.transpose(layered, (2, 0, 1, 3)).reshape(col_count, columns_here, width)
        return returning, "col", None

    def fifth(arrived):
        middle = jnp.einsum("sa,ks->ka", arrived.reshape(NT, width), theta_forward, precision=HIGH)
        return middle.reshape(row_count, kt_local, width), "row", None

    def sixth(arrived):
        shaped = arrived.reshape(row_count, kt_local, rows_here, kz_local)
        ordered = jnp.transpose(shaped, (1, 3, 0, 2)).reshape(kt_local, kz_local, NR)
        return jnp.einsum("tzj,kj->tzk", ordered, radial_forward, precision=HIGH)

    (c0,) = exchange(5, fourth(0))
    c1, d0 = exchange(6, fourth(1), fifth(c0))
    c2, d1 = exchange(7, fourth(2), fifth(c1))
    (d2,) = exchange(8, fifth(c2))
    return jnp.stack([sixth(d0), sixth(d1), sixth(d2)])


def solution(mesh):
    placed = (P(None, "row", "col", None), P(None, "row", "col", None))
    return jax.shard_map(
        per_device,
        mesh=mesh,
        in_specs=placed,
        out_specs=P(None, "row", "col", None),
        check_vma=False,
    )
```
